32 devices in a mesh: groups: 2 (over x), blk: 16 (over z, y, core).
Axes of the slice: x: 2, y: 2, z: 4, core: 2. Of those that a mesh axis runs over, the one named last changes fastest.
Arguments:
- hidden: bfloat16 [8192, 14336], P(('groups', 'blk')), parts along dimension 0, may hold values from -170 to 170
- cotangent: bfloat16 [8192, 4096], P(('groups', 'blk')), parts along dimension 0, may hold values from -170 to 170
- proj_in: bfloat16 [14336, 64], replicated, may hold values from -0.046875 to 0.046875
- proj_out: bfloat16 [4096, 64], replicated, may hold values from -0.09375 to 0.09375
- token_counts: int32 [128], P(('groups', 'blk')), parts along dimension 0, may hold values from 16 to 64
- loss_mask: int32 [8192], P(('groups', 'blk')), parts along dimension 0, may hold values 0 or 1
- prompt_ids: int32 [128], P('groups'), parts along dimension 0, may hold values from 0 to 15
Outputs:
- similarity: float32 [128, 64], P(('groups', 'blk')), parts along dimension 0
- self_norm: float32 [128], P(('groups', 'blk')), parts along dimension 0
- dup_score: float32 [128], P(('groups', 'blk')), parts along dimension 0
The draws below stay inside these ranges and needn't reach their ends.
There are 2 independent parts, one for each index of `groups`. The reference program is written for one: setup_inputs(seed, part) draws one part's arguments, and reference() takes and returns one part's arrays. A program takes and returns all parts, laid end to end along the dimension named above; an argument that names none is the same for every part. Nothing has to cross between parts.
All inputs are finite; a program needn't handle non-finite values. No bound on the sum of `loss_mask` on one device may be relied on, other than what follows from the above.
Results may differ from the reference program's by a relative error of at most 0.012.
The reference program's roundings to bfloat16 on the way (of `example_grad` and `whitened`) count: a program that leaves them out, or rounds other values in their place, can miss the bound.
Values may be sent and summed in bfloat16 or wider, within the bound.
A program may use at most 64 MiB of HBM per device.

```python
import math
import jax
import jax.numpy as jnp
from jax import lax

D = 4096
FF = 14336
K = 64
TOK_EX = 64
EXAMPLES = 64
TOKENS = 4096


LOG_TEN = math.log(10.0)


def row_col_scales(key, num_rows, num_cols, rise_log):
    key_row, key_col = jax.random.split(key)
    position = jnp.arange(num_rows, dtype=jnp.float32) / num_rows
    row_scale = jnp.exp(jax.random.uniform(key_row, (num_rows,), jnp.float32, 0.0, LOG_TEN) + 0.5 * rise_log * position)
    col_scale = jnp.exp(jax.random.uniform(key_col, (num_cols,), jnp.float32, 0.0, LOG_TEN))
    return row_scale[:, None] * col_scale[None, :]


def draw_hidden(key, part):
    key = jax.random.fold_in(key, 11)
    key_scale, key_noise = jax.random.split(key, 2)
    scale_grid = row_col_scales(key_scale, TOKENS, FF, math.log(3.0))
    noise_field = jax.random.normal(key_noise, (TOKENS, FF), jnp.float32)
    return (jnp.clip(noise_field, -6.0, 6.0) * scale_grid * 0.1).astype(jnp.bfloat16)


def draw_cotangent(key, part):
    key = jax.random.fold_in(key, 12)
    key_scale, key_noise = jax.random.split(key, 2)
    scale_grid = row_col_scales(key_scale, TOKENS, D, math.log(3.0))
    noise_field = jax.random.normal(key_noise, (TOKENS, D), jnp.float32)
    return (jnp.clip(noise_field, -6.0, 6.0) * scale_grid * 0.1).astype(jnp.bfloat16)


def set_ends(result, stream_key, smallest, top_value):
    spot = [jax.random.randint(jax.random.fold_in(stream_key, axis), (), 0, length) for axis, length in enumerate(result.shape)]
    longest = result.shape.index(max(result.shape))
    neighbour = spot[:longest] + [(spot[longest] + 1) % result.shape[longest]] + spot[longest + 1:]
    return result.at[tuple(spot)].set(smallest).at[tuple(neighbour)].set(top_value)


def gaussian(rng, dims, deviation, reach, held_as=jnp.bfloat16):
    return jnp.clip(deviation * jax.random.normal(rng, dims, jnp.float32), -reach, reach).astype(held_as)


def setup_inputs(seed: int = 0, part: int = 0) -> dict:
    key_list = jax.random.split(jax.random.key(seed), 8)
    part_keys = jax.random.split(jax.random.fold_in(key_list[7], part), 8)
    return {
        "hidden": draw_hidden(jax.random.fold_in(jax.random.fold_in(key_list[7], part), 71), part),
        "cotangent": draw_cotangent(jax.random.fold_in(jax.random.fold_in(key_list[7], part), 71), part),
        "proj_in": gaussian(key_list[2], (FF, K), FF ** -0.5, 0.046875),
        "proj_out": gaussian(key_list[3], (D, K), D ** -0.5, 0.09375),
        "token_counts": set_ends(jax.random.randint(part_keys[4], (EXAMPLES,), TOK_EX // 4, TOK_EX + 1), jax.random.fold_in(part_keys[4], 1), TOK_EX // 4, TOK_EX).astype(jnp.int32),
        "loss_mask": set_ends((jax.random.randint(part_keys[5], (TOKENS,), 0, 4) < 3).astype(jnp.int32), jax.random.fold_in(part_keys[5], 1), 0, 1),
        "prompt_ids": set_ends(jax.random.randint(part_keys[6], (EXAMPLES,), 0, EXAMPLES // 4), jax.random.fold_in(part_keys[6], 1), 0, (EXAMPLES // 4) - 1).astype(jnp.int32),
    }


HIGHEST_MODE = lax.Precision.HIGHEST
DAMPING = 0.05
EPSILON = 1e-06
ROW_CONTRACT = (((1,), (1,)), ((), ()))

def factor_inverses(act_cov, grad_cov):
    rank_width = act_cov.shape[0]
    inverses = []
    for cov_matrix in (act_cov, grad_cov):
        identity = jnp.eye(rank_width, dtype=cov_matrix.dtype)
        damped = cov_matrix + (DAMPING * jnp.trace(cov_matrix) / rank_width + EPSILON) * identity
        lower_factor = jnp.linalg.cholesky(damped)
        inverses.append(jax.scipy.linalg.solve_triangular(lower_factor, identity, lower=True))
    return (inverses[0], inverses[1])

def whiten(raw_blocks, inv_grad, inv_act):
    rank_width = inv_act.shape[0]
    count_rows = raw_blocks.shape[0]
    grad_blocks = raw_blocks.astype(jnp.float32).reshape(count_rows, rank_width, rank_width)
    left_side = jnp.einsum('ab,ebc->eac', inv_grad, grad_blocks, precision=HIGHEST_MODE)
    whitened = jnp.einsum('eac,dc->ead', left_side, inv_act, precision=HIGHEST_MODE)
    return whitened.reshape(count_rows, rank_width * rank_width).astype(jnp.bfloat16)

def reference(hidden, cotangent, proj_in, proj_out, token_counts, loss_mask, prompt_ids):
    rank_width = proj_in.shape[1]
    examples = token_counts.shape[0]
    tokens = hidden.shape[0]
    tok_ex = tokens // examples
    act_proj = jnp.dot(hidden.astype(jnp.float32), proj_in.astype(jnp.float32), preferred_element_type=jnp.float32)
    grad_proj = jnp.dot(cotangent.astype(jnp.float32), proj_out.astype(jnp.float32), preferred_element_type=jnp.float32)
    slot_place = jnp.arange(tok_ex, dtype=jnp.int32)
    valid_slot = (slot_place[None, :] < token_counts[:, None]).astype(jnp.float32).reshape(tokens)
    masked_act = act_proj * valid_slot[:, None]
    masked_grad = grad_proj * (valid_slot * loss_mask.astype(jnp.float32))[:, None]
    act_cov = jnp.dot(masked_act.T, masked_act, precision=HIGHEST_MODE) / tokens
    grad_cov = jnp.dot(masked_grad.T, masked_grad, precision=HIGHEST_MODE) / tokens
    inv_act, inv_grad = factor_inverses(act_cov, grad_cov)
    row_scale = 1.0 / jnp.sqrt(rank_width * token_counts.astype(jnp.float32))
    outer_sum = jnp.einsum('etk,etl->ekl', masked_grad.reshape(examples, tok_ex, rank_width), act_proj.reshape(examples, tok_ex, rank_width), precision=HIGHEST_MODE)
    example_grad = (outer_sum * row_scale[:, None, None]).astype(jnp.bfloat16).reshape(examples, rank_width * rank_width)
    whitened = whiten(example_grad, inv_grad, inv_act)
    products = lax.dot_general(whitened.astype(jnp.float32), whitened.astype(jnp.float32), ROW_CONTRACT, preferred_element_type=jnp.float32)
    index_list = jnp.arange(examples, dtype=jnp.int32)
    similarity = jnp.where(index_list[:, None] == index_list[None, :], 0.0, products)
    self_norm = lax.optimization_barrier(jnp.sum(jnp.square(whitened.astype(jnp.float32)), axis=1)) / rank_width
    same_prompt = prompt_ids[:, None] == prompt_ids[None, :]
    dup_score = lax.optimization_barrier(jnp.sum(jnp.where(same_prompt, similarity * similarity, 0.0), axis=1))
    return (similarity, self_norm, dup_score)
```

```python
import functools

import jax
import jax.numpy as jnp
from jax import lax
from jax.experimental import pallas as pl
from jax.experimental.pallas import tpu as pltpu
from jax.sharding import PartitionSpec as P

HIGHEST_MODE = lax.Precision.HIGHEST
DAMPING = 0.05
EPSILON = 1e-06
MESH = pl.DeviceIdType.MESH
NN = (((1,), (0,)), ((), ()))
NT = (((1,), (1,)), ((), ()))
TN = (((0,), (0,)), ((), ()))
BLOCK_ROWS = 16


def dot32(a, b, dims=NN):
    return lax.dot_general(a, b, dims, precision=HIGHEST_MODE, preferred_element_type=jnp.float32)


def fold(square):
    half = square.shape[0] // 2
    return jnp.concatenate([square[:half], square[half:]], axis=1)


def unfold(folded):
    width = folded.shape[1] // 2
    return jnp.concatenate([folded[:, :width], folded[:, width:]], axis=0)


def spd_inverse(cov):
    width = cov.shape[0]
    row = lax.broadcasted_iota(jnp.int32, cov.shape, 0)
    col = lax.broadcasted_iota(jnp.int32, cov.shape, 1)
    on_diag = row == col
    trace = jnp.sum(jnp.sum(jnp.where(on_diag, cov, 0.0), axis=1, keepdims=True), axis=0, keepdims=True)
    shift = DAMPING * trace / width + EPSILON
    scale = 1.0 / (trace + shift)
    ident = jnp.where(on_diag, 1.0, 0.0)
    ratio = (cov + shift * ident) * scale
    low = 0.96 * DAMPING / (width + DAMPING)
    step = 2.0 / (1.0 + low)
    inverse = step * (2.0 * ident - step * ratio)
    ratio = step * (2.0 * ratio - step * dot32(ratio, ratio))
    low = 4.0 * low / (1.0 + low) ** 2
    while True:
        step = 2.0 / (1.0 + low)
        low = 4.0 * low / (1.0 + low) ** 2
        if 1.0 - low < 1e-5:
            inverse = step * (2.0 * inverse - step * dot32(inverse, ratio))
            return inverse * scale
        both = jnp.concatenate([ratio, inverse], axis=0)
        both = step * (2.0 * both - step * dot32(both, ratio))
        ratio, inverse = both[:width], both[width:]


def kernel(
    n, chunk,
    hidden, cotangent, proj_in, proj_out, counts, prompts, loss_row, prompt_row,
    sim_out, norm_out, dup_out,
    hid_v, cot_v, pin_v, pout_v, packed, half_send, half_recv, slots, inv_send, inv_recv, grads,
    in_sem, half_sem, slot_send, slot_recv, inv_sem, own_sem, grad_send, grad_recv, fwd_send, fwd_recv,
):
    chips = n // 2
    me = lax.axis_index("blk")
    group = lax.axis_index("groups")
    chip, core = me // 2, me % 2
    sibling = me + 1 - 2 * core
    tok, wide = hidden.shape
    rank = proj_in.shape[0]
    ex = counts.shape[0]
    tok_ex = tok // ex
    half = rank // 2

    def peer(shift):
        return lax.rem(chip + shift, chips)

    loads = []
    for source, weight, source_v, weight_v in (
        (cotangent, proj_out, cot_v, pout_v),
        (hidden, proj_in, hid_v, pin_v),
    ):
        for start in range(0, source.shape[1], chunk):
            cols = pl.ds(start, min(chunk, source.shape[1] - start))
            pair = []
            for from_ref, to_ref in ((weight, weight_v), (source, source_v)):
                copy = pltpu.make_async_copy(from_ref.at[:, cols], to_ref.at[:, cols], in_sem.at[2 * len(loads) + len(pair)])
                copy.start()
                pair.append(copy)
            loads.append((pair, cols, source_v, weight_v))

    barrier = pltpu.get_barrier_semaphore()
    pl.semaphore_signal(barrier, inc=1, device_id=(group, sibling), device_id_type=MESH)

    @pl.loop(1, chips)
    def _(shift):
        pl.semaphore_signal(barrier, inc=1, device_id=(group, 2 * peer(shift) + core), device_id_type=MESH)

    grad_t = jnp.zeros((rank, tok), jnp.float32)
    act = jnp.zeros((tok, rank), jnp.float32)
    for pair, cols, source_v, weight_v in loads:
        for copy in pair:
            copy.wait()
        if source_v is cot_v:
            grad_t += lax.dot_general(weight_v[:, cols], source_v[:, cols], NT, preferred_element_type=jnp.float32)
        else:
            act += lax.dot_general(source_v[:, cols], weight_v[:, cols], NT, preferred_element_type=jnp.float32)

    lane_tok = lax.broadcasted_iota(jnp.int32, (1, tok), 1)
    sub_tok = lax.broadcasted_iota(jnp.int32, (tok, 1), 0)
    lane_end = jnp.zeros((1, tok), jnp.int32)
    sub_end = jnp.zeros((tok, 1), jnp.int32)
    for e in range(ex):
        end = e * tok_ex + counts[e]
        lane_end = jnp.where(lane_tok // tok_ex == e, end, lane_end)
        sub_end = jnp.where(sub_tok // tok_ex == e, end, sub_end)
    lane_keep = jnp.where(lane_tok < lane_end, loss_row[...].astype(jnp.float32), 0.0)
    masked_grad = grad_t * lane_keep
    masked_act = jnp.where(sub_tok < sub_end, act, 0.0)

    act_part = fold(dot32(masked_act, masked_act, TN))
    grad_part = fold(dot32(masked_grad, masked_grad, NT))
    half_send[...] = jnp.where(core == 0, grad_part, act_part)
    pl.semaphore_wait(barrier, chips)
    half_copy = pltpu.make_async_remote_copy(
        src_ref=half_send, dst_ref=half_recv, send_sem=half_sem.at[0], recv_sem=half_sem.at[1],
        device_id=(group, sibling), device_id_type=MESH)
    half_copy.start()

    halves = []
    for h in range(2):
        rows = [
            jnp.where(lane_tok // tok_ex == e, masked_grad[h * half:(h + 1) * half], 0.0)
            for e in range(ex)
        ]
        summed = dot32(jnp.concatenate(rows, axis=0), act)
        parts = []
        for e in range(ex):
            count = jnp.full((1, 1), counts[e], jnp.int32).astype(jnp.float32)
            parts.append(summed[e * half:(e + 1) * half] * (1.0 / jnp.sqrt(rank * count)))
        halves.append(jnp.concatenate(parts, axis=0).astype(jnp.bfloat16).astype(jnp.float32))
    packed[...] = jnp.concatenate(halves, axis=1)
    per = BLOCK_ROWS // ex
    count_blocks = half // per

    def flat_rows():
        return jnp.concatenate(
            [packed[pl.ds(b, BLOCK_ROWS, stride=count_blocks), :] for b in range(count_blocks)], axis=1)

    own_rows = pl.ds(pl.multiple_of(me * BLOCK_ROWS, BLOCK_ROWS), BLOCK_ROWS)
    grads[own_rows, :] = flat_rows().astype(jnp.bfloat16)

    half_copy.wait()
    slots[chip] = jnp.where(core == 0, act_part, grad_part) + half_recv[...]

    def slot_copy(shift, source_chip, send, recv):
        return pltpu.make_async_remote_copy(
            src_ref=slots.at[source_chip], dst_ref=slots.at[source_chip], send_sem=send, recv_sem=recv,
            device_id=(group, 2 * peer(shift) + core), device_id_type=MESH)

    def grad_copy(owner, target, send, recv):
        rows = pl.ds(pl.multiple_of(owner * BLOCK_ROWS, BLOCK_ROWS), BLOCK_ROWS)
        return pltpu.make_async_remote_copy(
            src_ref=grads.at[rows, :], dst_ref=grads.at[rows, :], send_sem=send, recv_sem=recv,
            device_id=(group, target), device_id_type=MESH)

    @pl.loop(1, chips)
    def _(shift):
        slot_copy(shift, chip, slot_send.at[shift], slot_recv.at[shift]).start()

    grad_copy(me, sibling, own_sem.at[0], own_sem.at[1]).start()

    @pl.loop(1, chips)
    def _(shift):
        grad_copy(me, 2 * peer(shift) + core, grad_send.at[shift], grad_recv.at[shift]).start()

    @pl.loop(1, chips)
    def _(shift):
        slot_copy(shift, peer(chips - shift), slot_send.at[shift], slot_recv.at[shift]).wait_recv()

    total = slots[0]
    for k in range(1, chips):
        total += slots[k]
    tokens = tok * n
    inv_own = spd_inverse(unfold(total) * (1.0 / tokens))
    inv_send[...] = fold(inv_own)
    inv_copy = pltpu.make_async_remote_copy(
        src_ref=inv_send, dst_ref=inv_recv, send_sem=inv_sem.at[0], recv_sem=inv_sem.at[1],
        device_id=(group, sibling), device_id_type=MESH)
    inv_copy.start()

    @pl.loop(1, chips)
    def _(shift):
        owner = 2 * peer(chips - shift) + core
        grad_copy(owner, sibling, grad_send.at[shift], grad_recv.at[shift]).wait_recv()
        grad_copy(owner, sibling, fwd_send.at[shift], fwd_recv.at[shift]).start()

    inv_copy.wait()
    inv_other = unfold(inv_recv[...])
    inv_act = jnp.where(core == 0, inv_own, inv_other)
    inv_grad = jnp.where(core == 0, inv_other, inv_own)
    sides = [dot32(part, inv_act) for part in halves]
    for e in range(ex):
        rows = slice(e * half, (e + 1) * half)
        both = jnp.concatenate([sides[0][rows], sides[1][rows]], axis=0)
        packed[rows, :] = fold(dot32(inv_grad, both))
    scaled = flat_rows()
    terms = []
    for _ in range(3):
        term = scaled.astype(jnp.bfloat16)
        scaled = scaled - term.astype(jnp.float32)
        terms.append(term)
    lhs = jnp.concatenate(terms, axis=0)

    grad_copy(sibling, sibling, own_sem.at[0], own_sem.at[1]).wait_recv()

    @pl.loop(1, chips)
    def _(shift):
        owner = 2 * peer(chips - shift) + 1 - core
        grad_copy(owner, sibling, fwd_send.at[shift], fwd_recv.at[shift]).wait_recv()

    cross = lax.dot_general(lhs, grads[...], NT, preferred_element_type=jnp.float32)
    cross = cross[:BLOCK_ROWS] + cross[BLOCK_ROWS:2 * BLOCK_ROWS] + cross[2 * BLOCK_ROWS:]
    lanes = n * BLOCK_ROWS
    row = lax.broadcasted_iota(jnp.int32, (BLOCK_ROWS, lanes), 0)
    col = lax.broadcasted_iota(jnp.int32, (BLOCK_ROWS, lanes), 1)
    cross = jnp.where(row % per == col % per, cross, 0.0)
    cols_all = n * ex
    pick_row = lax.broadcasted_iota(jnp.int32, (lanes, cols_all), 0)
    pick_col = lax.broadcasted_iota(jnp.int32, (lanes, cols_all), 1)
    by_chunk = dot32(cross, jnp.where(pick_row // per == pick_col, 1.0, 0.0))
    products = jnp.concatenate(
        [jnp.sum(by_chunk[e * per:(e + 1) * per], axis=0, keepdims=True) for e in range(ex)], axis=0)

    row_ids = me * ex + lax.broadcasted_iota(jnp.int32, (ex, cols_all), 0)
    col_ids = lax.broadcasted_iota(jnp.int32, (ex, cols_all), 1)
    diagonal = row_ids == col_ids
    similarity = jnp.where(diagonal, 0.0, products)
    sim_out[...] = similarity
    norm_col = jnp.sum(jnp.where(diagonal, products, 0.0), axis=1, keepdims=True) / rank
    own_prompt = jnp.concatenate(
        [jnp.full((1, cols_all), prompts[me * ex + e], jnp.int32) for e in range(ex)], axis=0)
    same = own_prompt == prompt_row[...]
    dup_col = jnp.sum(jnp.where(same, similarity * similarity, 0.0), axis=1, keepdims=True)
    small_row = lax.broadcasted_iota(jnp.int32, (ex, ex), 0)
    small_col = lax.broadcasted_iota(jnp.int32, (ex, ex), 1)
    norm_out[...] = jnp.sum(jnp.where(small_row == small_col, norm_col, 0.0), axis=0, keepdims=True)
    dup_out[...] = jnp.sum(jnp.where(small_row == small_col, dup_col, 0.0), axis=0, keepdims=True)

    grad_copy(me, sibling, own_sem.at[0], own_sem.at[1]).wait_send()

    @pl.loop(1, chips)
    def _(shift):
        slot_copy(shift, chip, slot_send.at[shift], slot_recv.at[shift]).wait_send()
        grad_copy(me, 2 * peer(shift) + core, grad_send.at[shift], grad_recv.at[shift]).wait_send()
        owner = 2 * peer(chips - shift) + core
        grad_copy(owner, sibling, fwd_send.at[shift], fwd_recv.at[shift]).wait_send()


def local(n, hidden, cotangent, proj_in, proj_out, token_counts, loss_mask, prompt_ids):
    tok, wide = hidden.shape
    model = cotangent.shape[1]
    rank = proj_in.shape[1]
    ex = token_counts.shape[0]
    chips = n // 2
    chunk = 2048
    loads = -(-wide // chunk) + -(-model // chunk)
    folded = (rank // 2, 2 * rank)
    dma = pltpu.SemaphoreType.DMA
    f32, bf16 = jnp.float32, jnp.bfloat16
    whole = pl.BlockSpec(memory_space=pltpu.VMEM)
    scalars = pl.BlockSpec(memory_space=pltpu.SMEM)
    far = pl.BlockSpec(memory_space=pltpu.HBM)
    similarity, self_norm, dup_score = pl.pallas_call(
        functools.partial(kernel, n, chunk),
        out_shape=(
            jax.ShapeDtypeStruct((ex, n * ex), f32),
            jax.ShapeDtypeStruct((1, ex), f32),
            jax.ShapeDtypeStruct((1, ex), f32),
        ),
        in_specs=[far, far, far, far, scalars, scalars, whole, whole],
        out_specs=(whole, whole, whole),
        scratch_shapes=[
            pltpu.VMEM((tok, wide), bf16),
            pltpu.VMEM((tok, model), bf16),
            pltpu.VMEM((rank, wide), bf16),
            pltpu.VMEM((rank, model), bf16),
            pltpu.VMEM((ex * rank // 2, 2 * rank), f32),
            pltpu.VMEM(folded, f32),
            pltpu.VMEM(folded, f32),
            pltpu.VMEM((chips,) + folded, f32),
            pltpu.VMEM(folded, f32),
            pltpu.VMEM(folded, f32),
            pltpu.VMEM((n * BLOCK_ROWS, ex * rank * rank // BLOCK_ROWS), bf16),
            dma((2 * loads,)), dma((2,)), dma((chips,)), dma((chips,)), dma((2,)), dma((2,)),
            dma((chips,)), dma((chips,)), dma((chips,)), dma((chips,)),
        ],
        compiler_params=pltpu.CompilerParams(
            collective_id=0, has_side_effects=True, vmem_limit_bytes=48 * 1024 * 1024),
        cost_estimate=pl.CostEstimate(
            flops=2 * tok * (wide + model) * rank, bytes_accessed=2 * tok * (wide + model), transcendentals=0),
    )(hidden, cotangent, proj_in.T, proj_out.T, token_counts, prompt_ids,
      loss_mask.reshape(1, tok), prompt_ids.reshape(1, n * ex))
    return similarity, self_norm.reshape(ex), dup_score.reshape(ex)


def solution(mesh):
    placed = (
        P(("groups", "blk"), None),
        P(("groups", "blk"), None),
        P(),
        P(),
        P(("groups", "blk")),
        P(("groups", "blk")),
        P("groups"),
    )
    return jax.shard_map(
        functools.partial(local, mesh.shape["blk"]),
        mesh=mesh,
        in_specs=placed,
        out_specs=(P(("groups", "blk"), None), P(("groups", "blk")), P(("groups", "blk"))),
        check_vma=False,
    )
```

```python
import functools

import jax
import jax.numpy as jnp
from jax import lax
from jax.experimental import pallas as pl
from jax.experimental.pallas import tpu as pltpu
from jax.sharding import PartitionSpec as P

HIGHEST_MODE = lax.Precision.HIGHEST
DAMPING = 0.05
EPSILON = 1e-06
MESH = pl.DeviceIdType.MESH
NN = (((1,), (0,)), ((), ()))
NT = (((1,), (1,)), ((), ()))
TN = (((0,), (0,)), ((), ()))
BLOCK_ROWS = 16


def dot32(a, b, dims=NN):
    return lax.dot_general(a, b, dims, precision=HIGHEST_MODE, preferred_element_type=jnp.float32)


def fold(square):
    half = square.shape[0] // 2
    return jnp.concatenate([square[:half], square[half:]], axis=1)


def unfold(folded):
    width = folded.shape[1] // 2
    return jnp.concatenate([folded[:, :width], folded[:, width:]], axis=0)


def spd_inverse(cov):
    width = cov.shape[0]
    row = lax.broadcasted_iota(jnp.int32, cov.shape, 0)
    col = lax.broadcasted_iota(jnp.int32, cov.shape, 1)
    on_diag = row == col
    trace = jnp.sum(jnp.sum(jnp.where(on_diag, cov, 0.0), axis=1, keepdims=True), axis=0, keepdims=True)
    shift = DAMPING * trace / width + EPSILON
    scale = 1.0 / (trace + shift)
    ident = jnp.where(on_diag, 1.0, 0.0)
    ratio = (cov + shift * ident) * scale
    low = 0.96 * DAMPING / (width + DAMPING)
    step = 2.0 / (1.0 + low)
    inverse = step * (2.0 * ident - step * ratio)
    ratio = step * (2.0 * ratio - step * dot32(ratio, ratio))
    low = 4.0 * low / (1.0 + low) ** 2
    while True:
        step = 2.0 / (1.0 + low)
        low = 4.0 * low / (1.0 + low) ** 2
        if 1.0 - low < 1e-5:
            inverse = step * (2.0 * inverse - step * dot32(inverse, ratio))
            return inverse * scale
        both = jnp.concatenate([ratio, inverse], axis=0)
        both = step * (2.0 * both - step * dot32(both, ratio))
        ratio, inverse = both[:width], both[width:]


def kernel(
    n, chunk,
    hidden, cotangent, proj_in, proj_out, counts_far, loss_far, prompts_far,
    sim_out, norm_out, dup_out,
    hid_v, cot_v, pin_v, pout_v, packed, half_send, half_recv, slots, inv_send, inv_recv, grads,
    counts, prompts, loss_row, prompt_row,
    in_sem, small_sem, half_sem, slot_send, slot_recv, inv_sem, own_sem, grad_send, grad_recv, fwd_send, fwd_recv,
):
    chips = n // 2
    me = lax.axis_index("blk")
    group = lax.axis_index("groups")
    chip, core = me // 2, me % 2
    sibling = me + 1 - 2 * core
    tok, wide = hidden.shape
    rank = proj_in.shape[0]
    ex = counts_far.shape[0]
    tok_ex = tok // ex
    half = rank // 2

    def peer(shift):
        return lax.rem(chip + shift, chips)

    loads = []
    for source, weight, source_v, weight_v in (
        (cotangent, proj_out, cot_v, pout_v),
        (hidden, proj_in, hid_v, pin_v),
    ):
        for start in range(0, source.shape[1], chunk):
            cols = pl.ds(start, min(chunk, source.shape[1] - start))
            pair = []
            for from_ref, to_ref in ((weight, weight_v), (source, source_v)):
                copy = pltpu.make_async_copy(from_ref.at[:, cols], to_ref.at[:, cols], in_sem.at[2 * len(loads) + len(pair)])
                copy.start()
                pair.append(copy)
            loads.append((pair, cols, source_v, weight_v))

    small = []
    for from_ref, to_ref in (
        (counts_far, counts), (loss_far, loss_row.at[0]), (prompts_far, prompts), (prompts_far, prompt_row.at[0]),
    ):
        copy = pltpu.make_async_copy(from_ref, to_ref, small_sem.at[len(small)])
        copy.start()
        small.append(copy)

    barrier = pltpu.get_barrier_semaphore()
    pl.semaphore_signal(barrier, inc=1, device_id=(group, sibling), device_id_type=MESH)

    @pl.loop(1, chips)
    def _(shift):
        pl.semaphore_signal(barrier, inc=1, device_id=(group, 2 * peer(shift) + core), device_id_type=MESH)

    grad_t = jnp.zeros((rank, tok), jnp.float32)
    act = jnp.zeros((tok, rank), jnp.float32)
    for pair, cols, source_v, weight_v in loads:
        for copy in pair:
            copy.wait()
        if source_v is cot_v:
            grad_t += lax.dot_general(weight_v[:, cols], source_v[:, cols], NT, preferred_element_type=jnp.float32)
        else:
            act += lax.dot_general(source_v[:, cols], weight_v[:, cols], NT, preferred_element_type=jnp.float32)

    for copy in small:
        copy.wait()
    lane_tok = lax.broadcasted_iota(jnp.int32, (1, tok), 1)
    sub_tok = lax.broadcasted_iota(jnp.int32, (tok, 1), 0)
    lane_end = jnp.zeros((1, tok), jnp.int32)
    sub_end = jnp.zeros((tok, 1), jnp.int32)
    for e in range(ex):
        end = e * tok_ex + counts[e]
        lane_end = jnp.where(lane_tok // tok_ex == e, end, lane_end)
        sub_end = jnp.where(sub_tok // tok_ex == e, end, sub_end)
    lane_keep = jnp.where(lane_tok < lane_end, loss_row[...].astype(jnp.float32), 0.0)
    masked_grad = grad_t * lane_keep
    masked_act = jnp.where(sub_tok < sub_end, act, 0.0)

    act_part = fold(dot32(masked_act, masked_act, TN))
    grad_part = fold(dot32(masked_grad, masked_grad, NT))
    half_send[...] = jnp.where(core == 0, grad_part, act_part)
    pl.semaphore_wait(barrier, chips)
    half_copy = pltpu.make_async_remote_copy(
        src_ref=half_send, dst_ref=half_recv, send_sem=half_sem.at[0], recv_sem=half_sem.at[1],
        device_id=(group, sibling), device_id_type=MESH)
    half_copy.start()

    halves = []
    for h in range(2):
        rows = [
            jnp.where(lane_tok // tok_ex == e, masked_grad[h * half:(h + 1) * half], 0.0)
            for e in range(ex)
        ]
        summed = dot32(jnp.concatenate(rows, axis=0), act)
        parts = []
        for e in range(ex):
            count = jnp.full((1, 1), counts[e], jnp.int32).astype(jnp.float32)
            parts.append(summed[e * half:(e + 1) * half] * (1.0 / jnp.sqrt(rank * count)))
        halves.append(jnp.concatenate(parts, axis=0).astype(jnp.bfloat16).astype(jnp.float32))
    packed[...] = jnp.concatenate(halves, axis=1)
    per = BLOCK_ROWS // ex
    count_blocks = half // per

    def flat_rows():
        return jnp.concatenate(
            [packed[pl.ds(b, BLOCK_ROWS, stride=count_blocks), :] for b in range(count_blocks)], axis=1)

    own_rows = pl.ds(pl.multiple_of(me * BLOCK_ROWS, BLOCK_ROWS), BLOCK_ROWS)
    grads[own_rows, :] = flat_rows().astype(jnp.bfloat16)

    half_copy.wait()
    slots[chip] = jnp.where(core == 0, act_part, grad_part) + half_recv[...]

    def slot_copy(shift, source_chip, send, recv):
        return pltpu.make_async_remote_copy(
            src_ref=slots.at[source_chip], dst_ref=slots.at[source_chip], send_sem=send, recv_sem=recv,
            device_id=(group, 2 * peer(shift) + core), device_id_type=MESH)

    def grad_copy(owner, target, send, recv):
        rows = pl.ds(pl.multiple_of(owner * BLOCK_ROWS, BLOCK_ROWS), BLOCK_ROWS)
        return pltpu.make_async_remote_copy(
            src_ref=grads.at[rows, :], dst_ref=grads.at[rows, :], send_sem=send, recv_sem=recv,
            device_id=(group, target), device_id_type=MESH)

    @pl.loop(1, chips)
    def _(shift):
        slot_copy(shift, chip, slot_send.at[shift], slot_recv.at[shift]).start()

    grad_copy(me, sibling, own_sem.at[0], own_sem.at[1]).start()

    @pl.loop(1, chips)
    def _(shift):
        grad_copy(me, 2 * peer(shift) + core, grad_send.at[shift], grad_recv.at[shift]).start()

    @pl.loop(1, chips)
    def _(shift):
        slot_copy(shift, peer(chips - shift), slot_send.at[shift], slot_recv.at[shift]).wait_recv()

    total = slots[0]
    for k in range(1, chips):
        total += slots[k]
    tokens = tok * n
    inv_own = spd_inverse(unfold(total) * (1.0 / tokens))
    inv_send[...] = fold(inv_own)
    inv_copy = pltpu.make_async_remote_copy(
        src_ref=inv_send, dst_ref=inv_recv, send_sem=inv_sem.at[0], recv_sem=inv_sem.at[1],
        device_id=(group, sibling), device_id_type=MESH)
    inv_copy.start()

    @pl.loop(1, chips)
    def _(shift):
        owner = 2 * peer(chips - shift) + core
        grad_copy(owner, sibling, grad_send.at[shift], grad_recv.at[shift]).wait_recv()
        grad_copy(owner, sibling, fwd_send.at[shift], fwd_recv.at[shift]).start()

    inv_copy.wait()
    inv_other = unfold(inv_recv[...])
    inv_act = jnp.where(core == 0, inv_own, inv_other)
    inv_grad = jnp.where(core == 0, inv_other, inv_own)
    sides = [dot32(part, inv_act) for part in halves]
    for e in range(ex):
        rows = slice(e * half, (e + 1) * half)
        both = jnp.concatenate([sides[0][rows], sides[1][rows]], axis=0)
        packed[rows, :] = fold(dot32(inv_grad, both))
    scaled = flat_rows()
    terms = []
    for _ in range(3):
        term = scaled.astype(jnp.bfloat16)
        scaled = scaled - term.astype(jnp.float32)
        terms.append(term)
    lhs = jnp.concatenate(terms, axis=0)

    grad_copy(sibling, sibling, own_sem.at[0], own_sem.at[1]).wait_recv()

    @pl.loop(1, chips)
    def _(shift):
        owner = 2 * peer(chips - shift) + 1 - core
        grad_copy(owner, sibling, fwd_send.at[shift], fwd_recv.at[shift]).wait_recv()

    cross = lax.dot_general(lhs, grads[...], NT, preferred_element_type=jnp.float32)
    cross = cross[:BLOCK_ROWS] + cross[BLOCK_ROWS:2 * BLOCK_ROWS] + cross[2 * BLOCK_ROWS:]
    lanes = n * BLOCK_ROWS
    row = lax.broadcasted_iota(jnp.int32, (BLOCK_ROWS, lanes), 0)
    col = lax.broadcasted_iota(jnp.int32, (BLOCK_ROWS, lanes), 1)
    cross = jnp.where(row % per == col % per, cross, 0.0)
    cols_all = n * ex
    pick_row = lax.broadcasted_iota(jnp.int32, (lanes, cols_all), 0)
    pick_col = lax.broadcasted_iota(jnp.int32, (lanes, cols_all), 1)
    by_chunk = dot32(cross, jnp.where(pick_row // per == pick_col, 1.0, 0.0))
    products = jnp.concatenate(
        [jnp.sum(by_chunk[e * per:(e + 1) * per], axis=0, keepdims=True) for e in range(ex)], axis=0)

    row_ids = me * ex + lax.broadcasted_iota(jnp.int32, (ex, cols_all), 0)
    col_ids = lax.broadcasted_iota(jnp.int32, (ex, cols_all), 1)
    diagonal = row_ids == col_ids
    similarity = jnp.where(diagonal, 0.0, products)
    sim_out[...] = similarity
    norm_col = jnp.sum(jnp.where(diagonal, products, 0.0), axis=1, keepdims=True) / rank
    own_prompt = jnp.concatenate(
        [jnp.full((1, cols_all), prompts[me * ex + e], jnp.int32) for e in range(ex)], axis=0)
    same = own_prompt == prompt_row[...]
    dup_col = jnp.sum(jnp.where(same, similarity * similarity, 0.0), axis=1, keepdims=True)
    small_row = lax.broadcasted_iota(jnp.int32, (ex, ex), 0)
    small_col = lax.broadcasted_iota(jnp.int32, (ex, ex), 1)
    norm_out[...] = jnp.sum(jnp.where(small_row == small_col, norm_col, 0.0), axis=0, keepdims=True)
    dup_out[...] = jnp.sum(jnp.where(small_row == small_col, dup_col, 0.0), axis=0, keepdims=True)

    grad_copy(me, sibling, own_sem.at[0], own_sem.at[1]).wait_send()

    @pl.loop(1, chips)
    def _(shift):
        slot_copy(shift, chip, slot_send.at[shift], slot_recv.at[shift]).wait_send()
        grad_copy(me, 2 * peer(shift) + core, grad_send.at[shift], grad_recv.at[shift]).wait_send()
        owner = 2 * peer(chips - shift) + core
        grad_copy(owner, sibling, fwd_send.at[shift], fwd_recv.at[shift]).wait_send()


def local(n, hidden, cotangent, proj_in, proj_out, token_counts, loss_mask, prompt_ids):
    tok, wide = hidden.shape
    model = cotangent.shape[1]
    rank = proj_in.shape[1]
    ex = token_counts.shape[0]
    chips = n // 2
    chunk = 2048
    loads = -(-wide // chunk) + -(-model // chunk)
    folded = (rank // 2, 2 * rank)
    dma = pltpu.SemaphoreType.DMA
    f32, bf16 = jnp.float32, jnp.bfloat16
    whole = pl.BlockSpec(memory_space=pltpu.VMEM)
    far = pl.BlockSpec(memory_space=pltpu.HBM)
    similarity, self_norm, dup_score = pl.pallas_call(
        functools.partial(kernel, n, chunk),
        out_shape=(
            jax.ShapeDtypeStruct((ex, n * ex), f32),
            jax.ShapeDtypeStruct((1, ex), f32),
            jax.ShapeDtypeStruct((1, ex), f32),
        ),
        in_specs=[far] * 7,
        out_specs=(whole, whole, whole),
        scratch_shapes=[
            pltpu.VMEM((tok, wide), bf16),
            pltpu.VMEM((tok, model), bf16),
            pltpu.VMEM((rank, wide), bf16),
            pltpu.VMEM((rank, model), bf16),
            pltpu.VMEM((ex * rank // 2, 2 * rank), f32),
            pltpu.VMEM(folded, f32),
            pltpu.VMEM(folded, f32),
            pltpu.VMEM((chips,) + folded, f32),
            pltpu.VMEM(folded, f32),
            pltpu.VMEM(folded, f32),
            pltpu.VMEM((n * BLOCK_ROWS, ex * rank * rank // BLOCK_ROWS), bf16),
            pltpu.SMEM((ex,), jnp.int32),
            pltpu.SMEM((n * ex,), jnp.int32),
            pltpu.VMEM((1, tok), jnp.int32),
            pltpu.VMEM((1, n * ex), jnp.int32),
            dma((2 * loads,)), dma((4,)), dma((2,)), dma((chips,)), dma((chips,)), dma((2,)), dma((2,)),
            dma((chips,)), dma((chips,)), dma((chips,)), dma((chips,)),
        ],
        compiler_params=pltpu.CompilerParams(
            collective_id=0, has_side_effects=True, vmem_limit_bytes=60 * 1024 * 1024),
        cost_estimate=pl.CostEstimate(
            flops=2 * tok * (wide + model) * rank, bytes_accessed=2 * tok * (wide + model), transcendentals=0),
    )(hidden, cotangent, proj_in.T, proj_out.T, token_counts, loss_mask, prompt_ids)
    return similarity, self_norm.reshape(ex), dup_score.reshape(ex)


def solution(mesh):
    placed = (
        P(("groups", "blk"), None),
        P(("groups", "blk"), None),
        P(),
        P(),
        P(("groups", "blk")),
        P(("groups", "blk")),
        P("groups"),
    )
    return jax.shard_map(
        functools.partial(local, mesh.shape["blk"]),
        mesh=mesh,
        in_specs=placed,
        out_specs=(P(("groups", "blk"), None), P(("groups", "blk")), P(("groups", "blk"))),
        check_vma=False,
    )
```

```python
import functools

import jax
import jax.numpy as jnp
from jax import lax
from jax.experimental import pallas as pl
from jax.experimental.pallas import tpu as pltpu
from jax.sharding import PartitionSpec as P

HIGHEST_MODE = lax.Precision.HIGHEST
DAMPING = 0.05
EPSILON = 1e-06
MESH = pl.DeviceIdType.MESH
NN = (((1,), (0,)), ((), ()))
NT = (((1,), (1,)), ((), ()))
TN = (((0,), (0,)), ((), ()))
BLOCK_ROWS = 16


def dot32(a, b, dims=NN):
    return lax.dot_general(a, b, dims, precision=HIGHEST_MODE, preferred_element_type=jnp.float32)


def fold(square):
    half = square.shape[0] // 2
    return jnp.concatenate([square[:half], square[half:]], axis=1)


def unfold(folded):
    width = folded.shape[1] // 2
    return jnp.concatenate([folded[:, :width], folded[:, width:]], axis=0)


def spd_inverse(cov):
    width = cov.shape[0]
    row = lax.broadcasted_iota(jnp.int32, cov.shape, 0)
    col = lax.broadcasted_iota(jnp.int32, cov.shape, 1)
    on_diag = row == col
    trace = jnp.sum(jnp.sum(jnp.where(on_diag, cov, 0.0), axis=1, keepdims=True), axis=0, keepdims=True)
    shift = DAMPING * trace / width + EPSILON
    scale = 1.0 / (trace + shift)
    ident = jnp.where(on_diag, 1.0, 0.0)
    ratio = (cov + shift * ident) * scale
    low = 0.96 * DAMPING / (width + DAMPING)
    step = 2.0 / (1.0 + low)
    inverse = step * (2.0 * ident - step * ratio)
    ratio = step * (2.0 * ratio - step * dot32(ratio, ratio))
    low = 4.0 * low / (1.0 + low) ** 2
    while True:
        step = 2.0 / (1.0 + low)
        low = 4.0 * low / (1.0 + low) ** 2
        if 1.0 - low < 1e-5:
            inverse = step * (2.0 * inverse - step * dot32(inverse, ratio))
            return inverse * scale
        both = jnp.concatenate([ratio, inverse], axis=0)
        both = step * (2.0 * both - step * dot32(both, ratio))
        ratio, inverse = both[:width], both[width:]


def kernel(
    n, chunk,
    hidden, cotangent, proj_in, proj_out, counts_far, loss_far, prompts_far,
    sim_out, norm_out, dup_out,
    hid_v, cot_v, pin_v, pout_v, packed, half_send, half_recv, slots, inv_send, inv_recv, grads,
    counts, prompts, loss_row, prompt_row,
    in_sem, small_sem, half_sem, slot_send, slot_recv, inv_sem, own_sem, grad_send, grad_recv, fwd_send, fwd_recv,
):
    chips = n // 2
    me = lax.axis_index("blk")
    group = lax.axis_index("groups")
    chip, core = me // 2, me % 2
    sibling = me + 1 - 2 * core
    tok, wide = hidden.shape
    rank = proj_in.shape[0]
    ex = counts_far.shape[0]
    tok_ex = tok // ex
    half = rank // 2

    def peer(shift):
        return lax.rem(chip + shift, chips)

    loads = []
    for source, weight, source_v, weight_v in (
        (cotangent, proj_out, cot_v, pout_v),
        (hidden, proj_in, hid_v, pin_v),
    ):
        for start in range(0, source.shape[1], chunk):
            cols = pl.ds(start, min(chunk, source.shape[1] - start))
            pair = []
            for from_ref, to_ref in ((weight, weight_v), (source, source_v)):
                copy = pltpu.make_async_copy(from_ref.at[:, cols], to_ref.at[:, cols], in_sem.at[2 * len(loads) + len(pair)])
                copy.start()
                pair.append(copy)
            loads.append((pair, cols, source_v, weight_v))

    small = []
    for from_ref, to_ref in (
        (counts_far, counts), (loss_far, loss_row.at[0]), (prompts_far, prompts), (prompts_far, prompt_row.at[0]),
    ):
        copy = pltpu.make_async_copy(from_ref, to_ref, small_sem.at[len(small)])
        copy.start()
        small.append(copy)

    barrier = pltpu.get_barrier_semaphore()
    pl.semaphore_signal(barrier, inc=1, device_id=(group, sibling), device_id_type=MESH)

    @pl.loop(1, chips)
    def _(shift):
        pl.semaphore_signal(barrier, inc=1, device_id=(group, 2 * peer(shift) + core), device_id_type=MESH)

    grad_t = jnp.zeros((rank, tok), jnp.float32)
    act = jnp.zeros((tok, rank), jnp.float32)
    for pair, cols, source_v, weight_v in loads:
        for copy in pair:
            copy.wait()
        if source_v is cot_v:
            grad_t += lax.dot_general(weight_v[:, cols], source_v[:, cols], NT, preferred_element_type=jnp.float32)
        else:
            act += lax.dot_general(source_v[:, cols], weight_v[:, cols], NT, preferred_element_type=jnp.float32)

    for copy in small:
        copy.wait()
    lane_tok = lax.broadcasted_iota(jnp.int32, (1, tok), 1)
    sub_tok = lax.broadcasted_iota(jnp.int32, (tok, 1), 0)
    lane_end = jnp.zeros((1, tok), jnp.int32)
    sub_end = jnp.zeros((tok, 1), jnp.int32)
    for e in range(ex):
        end = e * tok_ex + counts[e]
        lane_end = jnp.where(lane_tok // tok_ex == e, end, lane_end)
        sub_end = jnp.where(sub_tok // tok_ex == e, end, sub_end)
    lane_keep = jnp.where(lane_tok < lane_end, loss_row[...].astype(jnp.float32), 0.0)
    masked_grad = grad_t * lane_keep
    masked_act = jnp.where(sub_tok < sub_end, act, 0.0)

    act_part = fold(dot32(masked_act, masked_act, TN))
    grad_part = fold(dot32(masked_grad, masked_grad, NT))
    half_send[...] = jnp.where(core == 0, grad_part, act_part)
    pl.semaphore_wait(barrier, chips)
    half_copy = pltpu.make_async_remote_copy(
        src_ref=half_send, dst_ref=half_recv, send_sem=half_sem.at[0], recv_sem=half_sem.at[1],
        device_id=(group, sibling), device_id_type=MESH)
    half_copy.start()

    halves = []
    for h in range(2):
        rows = [
            jnp.where(lane_tok // tok_ex == e, masked_grad[h * half:(h + 1) * half], 0.0)
            for e in range(ex)
        ]
        summed = dot32(jnp.concatenate(rows, axis=0), act)
        parts = []
        for e in range(ex):
            count = jnp.full((1, 1), counts[e], jnp.int32).astype(jnp.float32)
            parts.append(summed[e * half:(e + 1) * half] * (1.0 / jnp.sqrt(rank * count)))
        halves.append(jnp.concatenate(parts, axis=0).astype(jnp.bfloat16).astype(jnp.float32))
    packed[...] = jnp.concatenate(halves, axis=1)
    per = BLOCK_ROWS // ex
    count_blocks = half // per

    def flat_rows():
        return jnp.concatenate(
            [packed[pl.ds(b, BLOCK_ROWS, stride=count_blocks), :] for b in range(count_blocks)], axis=1)

    own_rows = pl.ds(pl.multiple_of(me * BLOCK_ROWS, BLOCK_ROWS), BLOCK_ROWS)
    grads[own_rows, :] = flat_rows().astype(jnp.bfloat16)

    half_copy.wait()
    slots[chip] = jnp.where(core == 0, act_part, grad_part) + half_recv[...]

    def slot_copy(shift, source_chip, send, recv):
        return pltpu.make_async_remote_copy(
            src_ref=slots.at[source_chip], dst_ref=slots.at[source_chip], send_sem=send, recv_sem=recv,
            device_id=(group, 2 * peer(shift) + core), device_id_type=MESH)

    def grad_copy(owner, target, send, recv):
        rows = pl.ds(pl.multiple_of(owner * BLOCK_ROWS, BLOCK_ROWS), BLOCK_ROWS)
        return pltpu.make_async_remote_copy(
            src_ref=grads.at[rows, :], dst_ref=grads.at[rows, :], send_sem=send, recv_sem=recv,
            device_id=(group, target), device_id_type=MESH)

    @pl.loop(1, chips)
    def _(shift):
        slot_copy(shift, chip, slot_send.at[shift], slot_recv.at[shift]).start()

    grad_copy(me, sibling, own_sem.at[0], own_sem.at[1]).start()

    @pl.loop(1, chips)
    def _(shift):
        grad_copy(me, 2 * peer(shift) + core, grad_send.at[shift], grad_recv.at[shift]).start()

    @pl.loop(1, chips)
    def _(shift):
        slot_copy(shift, peer(chips - shift), slot_send.at[shift], slot_recv.at[shift]).wait_recv()

    total = slots[0]
    for k in range(1, chips):
        total += slots[k]
    tokens = tok * n
    inv_own = spd_inverse(unfold(total) * (1.0 / tokens))
    inv_send[...] = fold(inv_own)
    inv_copy = pltpu.make_async_remote_copy(
        src_ref=inv_send, dst_ref=inv_recv, send_sem=inv_sem.at[0], recv_sem=inv_sem.at[1],
        device_id=(group, sibling), device_id_type=MESH)
    inv_copy.start()

    @pl.loop(1, chips)
    def _(shift):
        owner = 2 * peer(chips - shift) + core
        grad_copy(owner, sibling, grad_send.at[shift], grad_recv.at[shift]).wait_recv()
        grad_copy(owner, sibling, fwd_send.at[shift], fwd_recv.at[shift]).start()

    inv_copy.wait()
    inv_other = unfold(inv_recv[...])
    inv_act = jnp.where(core == 0, inv_own, inv_other)
    inv_grad = jnp.where(core == 0, inv_other, inv_own)
    sides = [dot32(part, inv_act) for part in halves]
    for e in range(ex):
        rows = slice(e * half, (e + 1) * half)
        both = jnp.concatenate([sides[0][rows], sides[1][rows]], axis=0)
        packed[rows, :] = fold(dot32(inv_grad, both))
    scaled = flat_rows()
    terms = []
    for _ in range(3):
        term = scaled.astype(jnp.bfloat16)
        scaled = scaled - term.astype(jnp.float32)
        terms.append(term)
    lhs = jnp.concatenate(terms, axis=0)

    grad_copy(sibling, sibling, own_sem.at[0], own_sem.at[1]).wait_recv()

    @pl.loop(1, chips)
    def _(shift):
        owner = 2 * peer(chips - shift) + 1 - core
        grad_copy(owner, sibling, fwd_send.at[shift], fwd_recv.at[shift]).wait_recv()

    cross = lax.dot_general(lhs, grads[...], NT, preferred_element_type=jnp.float32)
    cross = cross[:BLOCK_ROWS] + cross[BLOCK_ROWS:2 * BLOCK_ROWS] + cross[2 * BLOCK_ROWS:]
    lanes = n * BLOCK_ROWS
    row = lax.broadcasted_iota(jnp.int32, (BLOCK_ROWS, lanes), 0)
    col = lax.broadcasted_iota(jnp.int32, (BLOCK_ROWS, lanes), 1)
    cross = jnp.where(row % per == col % per, cross, 0.0)
    cols_all = n * ex
    pick_row = lax.broadcasted_iota(jnp.int32, (lanes, cols_all), 0)
    pick_col = lax.broadcasted_iota(jnp.int32, (lanes, cols_all), 1)
    by_chunk = dot32(cross, jnp.where(pick_row // per == pick_col, 1.0, 0.0))
    products = jnp.concatenate(
        [jnp.sum(by_chunk[e * per:(e + 1) * per], axis=0, keepdims=True) for e in range(ex)], axis=0)

    row_ids = me * ex + lax.broadcasted_iota(jnp.int32, (ex, cols_all), 0)
    col_ids = lax.broadcasted_iota(jnp.int32, (ex, cols_all), 1)
    diagonal = row_ids == col_ids
    similarity = jnp.where(diagonal, 0.0, products)
    sim_out[...] = similarity
    norm_col = jnp.sum(jnp.where(diagonal, products, 0.0), axis=1, keepdims=True) / rank
    own_prompt = jnp.concatenate(
        [jnp.full((1, cols_all), prompts[me * ex + e], jnp.int32) for e in range(ex)], axis=0)
    same = own_prompt == prompt_row[...]
    dup_col = jnp.sum(jnp.where(same, similarity * similarity, 0.0), axis=1, keepdims=True)
    small_row = lax.broadcasted_iota(jnp.int32, (ex, ex), 0)
    small_col = lax.broadcasted_iota(jnp.int32, (ex, ex), 1)
    norm_out[...] = jnp.sum(jnp.where(small_row == small_col, norm_col, 0.0), axis=0, keepdims=True)
    dup_out[...] = jnp.sum(jnp.where(small_row == small_col, dup_col, 0.0), axis=0, keepdims=True)

    grad_copy(me, sibling, own_sem.at[0], own_sem.at[1]).wait_send()

    @pl.loop(1, chips)
    def _(shift):
        slot_copy(shift, chip, slot_send.at[shift], slot_recv.at[shift]).wait_send()
        grad_copy(me, 2 * peer(shift) + core, grad_send.at[shift], grad_recv.at[shift]).wait_send()
        owner = 2 * peer(chips - shift) + core
        grad_copy(owner, sibling, fwd_send.at[shift], fwd_recv.at[shift]).wait_send()


def local(n, hidden, cotangent, proj_in, proj_out, token_counts, loss_mask, prompt_ids):
    tok, wide = hidden.shape
    model = cotangent.shape[1]
    rank = proj_in.shape[1]
    ex = token_counts.shape[0]
    chips = n // 2
    chunk = 2048
    loads = -(-wide // chunk) + -(-model // chunk)
    folded = (rank // 2, 2 * rank)
    dma = pltpu.SemaphoreType.DMA
    f32, bf16 = jnp.float32, jnp.bfloat16
    whole = pl.BlockSpec(memory_space=pltpu.VMEM)
    far = pl.BlockSpec(memory_space=pltpu.HBM)
    similarity, self_norm, dup_score = pl.pallas_call(
        functools.partial(kernel, n, chunk),
        out_shape=(
            jax.ShapeDtypeStruct((ex, n * ex), f32),
            jax.ShapeDtypeStruct((1, ex), f32),
            jax.ShapeDtypeStruct((1, ex), f32),
        ),
        in_specs=[far] * 7,
        out_specs=(whole, whole, whole),
        scratch_shapes=[
            pltpu.VMEM((tok, wide), bf16),
            pltpu.VMEM((tok, model), bf16),
            pltpu.VMEM((rank, wide), bf16),
            pltpu.VMEM((rank, model), bf16),
            pltpu.VMEM((ex * rank // 2, 2 * rank), f32),
            pltpu.VMEM(folded, f32),
            pltpu.VMEM(folded, f32),
            pltpu.VMEM((chips,) + folded, f32),
            pltpu.VMEM(folded, f32),
            pltpu.VMEM(folded, f32),
            pltpu.VMEM((n * BLOCK_ROWS, ex * rank * rank // BLOCK_ROWS), bf16),
            pltpu.SMEM((ex,), jnp.int32),
            pltpu.SMEM((n * ex,), jnp.int32),
            pltpu.VMEM((1, tok), jnp.int32),
            pltpu.VMEM((1, n * ex), jnp.int32),
            dma((2 * loads,)), dma((4,)), dma((2,)), dma((chips,)), dma((chips,)), dma((2,)), dma((2,)),
            dma((chips,)), dma((chips,)), dma((chips,)), dma((chips,)),
        ],
        compiler_params=pltpu.CompilerParams(
            collective_id=0, has_side_effects=True, vmem_limit_bytes=48 * 1024 * 1024),
        cost_estimate=pl.CostEstimate(
            flops=2 * tok * (wide + model) * rank, bytes_accessed=2 * tok * (wide + model), transcendentals=0),
    )(*[pltpu.with_memory_space_constraint(x, pltpu.HBM) for x in (
        hidden, cotangent, proj_in.T, proj_out.T, token_counts, loss_mask, prompt_ids)])
    return similarity, self_norm.reshape(ex), dup_score.reshape(ex)


def solution(mesh):
    placed = (
        P(("groups", "blk"), None),
        P(("groups", "blk"), None),
        P(),
        P(),
        P(("groups", "blk")),
        P(("groups", "blk")),
        P("groups"),
    )
    return jax.shard_map(
        functools.partial(local, mesh.shape["blk"]),
        mesh=mesh,
        in_specs=placed,
        out_specs=(P(("groups", "blk"), None), P(("groups", "blk")), P(("groups", "blk"))),
        check_vma=False,
    )
```

```python
import functools

import jax
import jax.numpy as jnp
from jax import lax
from jax.experimental import pallas as pl
from jax.experimental.pallas import tpu as pltpu
from jax.sharding import PartitionSpec as P

HIGHEST_MODE = lax.Precision.HIGHEST
DAMPING = 0.05
EPSILON = 1e-06
MESH = pl.DeviceIdType.MESH
NN = (((1,), (0,)), ((), ()))
NT = (((1,), (1,)), ((), ()))
TN = (((0,), (0,)), ((), ()))
BLOCK_ROWS = 16
SHARE_AFTER = 2


def plan(length, chunk):
    return [(start, min(chunk, length - start)) for start in range(0, length, chunk)]


def dot32(a, b, dims=NN):
    return lax.dot_general(a, b, dims, precision=HIGHEST_MODE, preferred_element_type=jnp.float32)


def fold(square):
    half = square.shape[0] // 2
    return jnp.concatenate([square[:half], square[half:]], axis=1)


def unfold(folded):
    width = folded.shape[1] // 2
    return jnp.concatenate([folded[:, :width], folded[:, width:]], axis=0)


def spd_inverse(cov):
    width = cov.shape[0]
    row = lax.broadcasted_iota(jnp.int32, cov.shape, 0)
    col = lax.broadcasted_iota(jnp.int32, cov.shape, 1)
    on_diag = row == col
    trace = jnp.sum(jnp.sum(jnp.where(on_diag, cov, 0.0), axis=1, keepdims=True), axis=0, keepdims=True)
    shift = DAMPING * trace / width + EPSILON
    scale = 1.0 / (trace + shift)
    ident = jnp.where(on_diag, 1.0, 0.0)
    ratio = (cov + shift * ident) * scale
    low = 0.96 * DAMPING / (width + DAMPING)
    step = 2.0 / (1.0 + low)
    inverse = step * (2.0 * ident - step * ratio)
    ratio = step * (2.0 * ratio - step * dot32(ratio, ratio))
    low = 4.0 * low / (1.0 + low) ** 2
    while True:
        step = 2.0 / (1.0 + low)
        low = 4.0 * low / (1.0 + low) ** 2
        if 1.0 - low < 1e-5:
            inverse = step * (2.0 * inverse - step * dot32(inverse, ratio))
            return inverse * scale
        both = jnp.concatenate([ratio, inverse], axis=0)
        both = step * (2.0 * both - step * dot32(both, ratio))
        ratio, inverse = both[:width], both[width:]


def kernel(
    n, chunk,
    hidden, cotangent, proj_in, proj_out, counts_far, loss_far, prompts_far,
    result,
    hid_v, cot_v, pin_v, pout_v, packed, half_send, half_recv, slots, inv_send, inv_recv, grads,
    counts, prompts, loss_row, prompt_row,
    in_sem, small_sem, half_sem, slot_send, slot_recv, inv_sem, own_sem, grad_send, grad_recv, fwd_send, fwd_recv,
):
    chips = n // 2
    me = lax.axis_index("blk")
    group = lax.axis_index("groups")
    chip, core = me // 2, me % 2
    sibling = me + 1 - 2 * core
    tok, wide = hidden.shape
    rank = proj_in.shape[0]
    ex = counts_far.shape[0]
    tok_ex = tok // ex
    half = rank // 2

    def peer(shift):
        return lax.rem(chip + shift, chips)

    loads = []
    for source, weight, source_v, weight_v in (
        (cotangent, proj_out, cot_v, pout_v),
        (hidden, proj_in, hid_v, pin_v),
    ):
        for start, size in plan(source.shape[1], chunk):
            cols = pl.ds(start, size)
            pair = []
            for from_ref, to_ref in ((weight, weight_v), (source, source_v)):
                copy = pltpu.make_async_copy(from_ref.at[:, cols], to_ref.at[:, cols], in_sem.at[2 * len(loads) + len(pair)])
                copy.start()
                pair.append(copy)
            loads.append((pair, cols, source_v, weight_v))

    small = []
    for from_ref, to_ref in (
        (counts_far, counts), (loss_far, loss_row.at[0]), (prompts_far, prompts), (prompts_far, prompt_row.at[0]),
    ):
        copy = pltpu.make_async_copy(from_ref, to_ref, small_sem.at[len(small)])
        copy.start()
        small.append(copy)

    barrier = pltpu.get_barrier_semaphore()
    pl.semaphore_signal(barrier, inc=1, device_id=(group, sibling), device_id_type=MESH)

    @pl.loop(1, chips)
    def _(shift):
        pl.semaphore_signal(barrier, inc=1, device_id=(group, 2 * peer(shift) + core), device_id_type=MESH)

    half_copy = pltpu.make_async_remote_copy(
        src_ref=half_send, dst_ref=half_recv, send_sem=half_sem.at[0], recv_sem=half_sem.at[1],
        device_id=(group, sibling), device_id_type=MESH)

    def slot_copy(shift, source_chip, send, recv):
        return pltpu.make_async_remote_copy(
            src_ref=slots.at[source_chip], dst_ref=slots.at[source_chip], send_sem=send, recv_sem=recv,
            device_id=(group, 2 * peer(shift) + core), device_id_type=MESH)

    def share(part):
        half_copy.wait_recv()
        slots[chip] = part + half_recv[...]

        @pl.loop(1, chips)
        def _(shift):
            slot_copy(shift, chip, slot_send.at[shift], slot_recv.at[shift]).start()

    grad_t = jnp.zeros((rank, tok), jnp.float32)
    for pair, cols, source_v, weight_v in loads:
        if source_v is cot_v:
            for copy in pair:
                copy.wait()
            grad_t += lax.dot_general(weight_v[:, cols], source_v[:, cols], NT, preferred_element_type=jnp.float32)

    for copy in small:
        copy.wait()
    lane_tok = lax.broadcasted_iota(jnp.int32, (1, tok), 1)
    sub_tok = lax.broadcasted_iota(jnp.int32, (tok, 1), 0)
    lane_end = jnp.zeros((1, tok), jnp.int32)
    sub_end = jnp.zeros((tok, 1), jnp.int32)
    for e in range(ex):
        end = e * tok_ex + counts[e]
        lane_end = jnp.where(lane_tok // tok_ex == e, end, lane_end)
        sub_end = jnp.where(sub_tok // tok_ex == e, end, sub_end)
    lane_keep = jnp.where(lane_tok < lane_end, loss_row[...].astype(jnp.float32), 0.0)
    masked_grad = grad_t * lane_keep
    grad_part = fold(dot32(masked_grad, masked_grad, NT))
    pl.semaphore_wait(barrier, chips)

    @pl.when(core == 0)
    def _():
        half_send[...] = grad_part
        half_copy.start()

    act = jnp.zeros((tok, rank), jnp.float32)
    count_hidden = 0
    for pair, cols, source_v, weight_v in loads:
        if source_v is hid_v:
            for copy in pair:
                copy.wait()
            act += lax.dot_general(source_v[:, cols], weight_v[:, cols], NT, preferred_element_type=jnp.float32)
            count_hidden += 1
            if count_hidden == SHARE_AFTER:
                @pl.when(core == 1)
                def _():
                    share(grad_part)

    masked_act = jnp.where(sub_tok < sub_end, act, 0.0)
    act_part = fold(dot32(masked_act, masked_act, TN))

    @pl.when(core == 1)
    def _():
        half_send[...] = act_part
        half_copy.start()

    halves = []
    for h in range(2):
        rows = [
            jnp.where(lane_tok // tok_ex == e, masked_grad[h * half:(h + 1) * half], 0.0)
            for e in range(ex)
        ]
        summed = dot32(jnp.concatenate(rows, axis=0), act)
        parts = []
        for e in range(ex):
            count = jnp.full((1, 1), counts[e], jnp.int32).astype(jnp.float32)
            parts.append(summed[e * half:(e + 1) * half] * (1.0 / jnp.sqrt(rank * count)))
        halves.append(jnp.concatenate(parts, axis=0).astype(jnp.bfloat16).astype(jnp.float32))
    packed[...] = jnp.concatenate(halves, axis=1)
    per = BLOCK_ROWS // ex
    count_blocks = half // per

    def flat_rows():
        return jnp.concatenate(
            [packed[pl.ds(b, BLOCK_ROWS, stride=count_blocks), :] for b in range(count_blocks)], axis=1)

    own_rows = pl.ds(pl.multiple_of(me * BLOCK_ROWS, BLOCK_ROWS), BLOCK_ROWS)
    grads[own_rows, :] = flat_rows().astype(jnp.bfloat16)

    @pl.when(core == 0)
    def _():
        share(act_part)

    def grad_copy(owner, target, send, recv):
        rows = pl.ds(pl.multiple_of(owner * BLOCK_ROWS, BLOCK_ROWS), BLOCK_ROWS)
        return pltpu.make_async_remote_copy(
            src_ref=grads.at[rows, :], dst_ref=grads.at[rows, :], send_sem=send, recv_sem=recv,
            device_id=(group, target), device_id_type=MESH)

    grad_copy(me, sibling, own_sem.at[0], own_sem.at[1]).start()

    @pl.loop(1, chips)
    def _(shift):
        grad_copy(me, 2 * peer(shift) + core, grad_send.at[shift], grad_recv.at[shift]).start()

    @pl.loop(1, chips)
    def _(shift):
        slot_copy(shift, peer(chips - shift), slot_send.at[shift], slot_recv.at[shift]).wait_recv()

    total = slots[0]
    for k in range(1, chips):
        total += slots[k]
    tokens = tok * n
    inv_own = spd_inverse(unfold(total) * (1.0 / tokens))
    inv_send[...] = fold(inv_own)
    inv_copy = pltpu.make_async_remote_copy(
        src_ref=inv_send, dst_ref=inv_recv, send_sem=inv_sem.at[0], recv_sem=inv_sem.at[1],
        device_id=(group, sibling), device_id_type=MESH)
    inv_copy.start()

    @pl.loop(1, chips)
    def _(shift):
        owner = 2 * peer(chips - shift) + core
        grad_copy(owner, sibling, grad_send.at[shift], grad_recv.at[shift]).wait_recv()
        grad_copy(owner, sibling, fwd_send.at[shift], fwd_recv.at[shift]).start()

    inv_copy.wait()
    inv_other = unfold(inv_recv[...])
    inv_act = jnp.where(core == 0, inv_own, inv_other)
    inv_grad = jnp.where(core == 0, inv_other, inv_own)
    sides = [dot32(part, inv_act) for part in halves]
    for e in range(ex):
        rows = slice(e * half, (e + 1) * half)
        both = jnp.concatenate([sides[0][rows], sides[1][rows]], axis=0)
        packed[rows, :] = fold(dot32(inv_grad, both))
    scaled = flat_rows()
    terms = []
    for _ in range(3):
        term = scaled.astype(jnp.bfloat16)
        scaled = scaled - term.astype(jnp.float32)
        terms.append(term)
    lhs = jnp.concatenate(terms, axis=0)

    grad_copy(sibling, sibling, own_sem.at[0], own_sem.at[1]).wait_recv()

    @pl.loop(1, chips)
    def _(shift):
        owner = 2 * peer(chips - shift) + 1 - core
        grad_copy(owner, sibling, fwd_send.at[shift], fwd_recv.at[shift]).wait_recv()

    cross = lax.dot_general(lhs, grads[...], NT, preferred_element_type=jnp.float32)
    cross = cross[:BLOCK_ROWS] + cross[BLOCK_ROWS:2 * BLOCK_ROWS] + cross[2 * BLOCK_ROWS:]
    lanes = n * BLOCK_ROWS
    row = lax.broadcasted_iota(jnp.int32, (BLOCK_ROWS, lanes), 0)
    col = lax.broadcasted_iota(jnp.int32, (BLOCK_ROWS, lanes), 1)
    cross = jnp.where(row % per == col % per, cross, 0.0)
    cols_all = n * ex
    pick_row = lax.broadcasted_iota(jnp.int32, (lanes, cols_all), 0)
    pick_col = lax.broadcasted_iota(jnp.int32, (lanes, cols_all), 1)
    by_chunk = dot32(cross, jnp.where(pick_row // per == pick_col, 1.0, 0.0))
    products = jnp.concatenate(
        [jnp.sum(by_chunk[e * per:(e + 1) * per], axis=0, keepdims=True) for e in range(ex)], axis=0)

    row_ids = me * ex + lax.broadcasted_iota(jnp.int32, (ex, cols_all), 0)
    col_ids = lax.broadcasted_iota(jnp.int32, (ex, cols_all), 1)
    diagonal = row_ids == col_ids
    similarity = jnp.where(diagonal, 0.0, products)
    norm_col = jnp.sum(jnp.where(diagonal, products, 0.0), axis=1, keepdims=True) / rank
    own_prompt = jnp.concatenate(
        [jnp.full((1, cols_all), prompts[me * ex + e], jnp.int32) for e in range(ex)], axis=0)
    same = own_prompt == prompt_row[...]
    dup_col = jnp.sum(jnp.where(same, similarity * similarity, 0.0), axis=1, keepdims=True)
    extra = lax.broadcasted_iota(jnp.int32, (ex, result.shape[1] - cols_all), 1)
    result[...] = jnp.concatenate(
        [similarity, jnp.where(extra == 0, norm_col, jnp.where(extra == 1, dup_col, 0.0))], axis=1)

    half_copy.wait_send()
    grad_copy(me, sibling, own_sem.at[0], own_sem.at[1]).wait_send()

    @pl.loop(1, chips)
    def _(shift):
        slot_copy(shift, chip, slot_send.at[shift], slot_recv.at[shift]).wait_send()
        grad_copy(me, 2 * peer(shift) + core, grad_send.at[shift], grad_recv.at[shift]).wait_send()
        owner = 2 * peer(chips - shift) + core
        grad_copy(owner, sibling, fwd_send.at[shift], fwd_recv.at[shift]).wait_send()


def local(n, hidden, cotangent, proj_in, proj_out, token_counts, loss_mask, prompt_ids):
    tok, wide = hidden.shape
    model = cotangent.shape[1]
    rank = proj_in.shape[1]
    ex = token_counts.shape[0]
    chips = n // 2
    chunk = 4096
    loads = len(plan(wide, chunk)) + len(plan(model, chunk))
    folded = (rank // 2, 2 * rank)
    dma = pltpu.SemaphoreType.DMA
    f32, bf16 = jnp.float32, jnp.bfloat16
    whole = pl.BlockSpec(memory_space=pltpu.VMEM)
    far = pl.BlockSpec(memory_space=pltpu.HBM)
    width = -(-(n * ex + 2) // 128) * 128
    packed = pl.pallas_call(
        functools.partial(kernel, n, chunk),
        out_shape=jax.ShapeDtypeStruct((ex, width), f32),
        in_specs=[far] * 7,
        out_specs=whole,
        scratch_shapes=[
            pltpu.VMEM((tok, wide), bf16),
            pltpu.VMEM((tok, model), bf16),
            pltpu.VMEM((rank, wide), bf16),
            pltpu.VMEM((rank, model), bf16),
            pltpu.VMEM((ex * rank // 2, 2 * rank), f32),
            pltpu.VMEM(folded, f32),
            pltpu.VMEM(folded, f32),
            pltpu.VMEM((chips,) + folded, f32),
            pltpu.VMEM(folded, f32),
            pltpu.VMEM(folded, f32),
            pltpu.VMEM((n * BLOCK_ROWS, ex * rank * rank // BLOCK_ROWS), bf16),
            pltpu.SMEM((ex,), jnp.int32),
            pltpu.SMEM((n * ex,), jnp.int32),
            pltpu.VMEM((1, tok), jnp.int32),
            pltpu.VMEM((1, n * ex), jnp.int32),
            dma((2 * loads,)), dma((4,)), dma((2,)), dma((chips,)), dma((chips,)), dma((2,)), dma((2,)),
            dma((chips,)), dma((chips,)), dma((chips,)), dma((chips,)),
        ],
        compiler_params=pltpu.CompilerParams(
            collective_id=0, has_side_effects=True, vmem_limit_bytes=48 * 1024 * 1024),
        cost_estimate=pl.CostEstimate(
            flops=2 * tok * (wide + model) * rank, bytes_accessed=2 * tok * (wide + model), transcendentals=0),
    )(*[pltpu.with_memory_space_constraint(x, pltpu.HBM) for x in (
        hidden, cotangent, proj_in.T, proj_out.T, token_counts, loss_mask, prompt_ids)])
    return packed[:, :n * ex], packed[:, n * ex], packed[:, n * ex + 1]


def solution(mesh):
    placed = (
        P(("groups", "blk"), None),
        P(("groups", "blk"), None),
        P(),
        P(),
        P(("groups", "blk")),
        P(("groups", "blk")),
        P("groups"),
    )
    return jax.shard_map(
        functools.partial(local, mesh.shape["blk"]),
        mesh=mesh,
        in_specs=placed,
        out_specs=(P(("groups", "blk"), None), P(("groups", "blk")), P(("groups", "blk"))),
        check_vma=False,
    )
```
